32 devices in a mesh: gx: 4 (over x, core), gy: 4 (over z), gz: 2 (over y).
Axes of the slice: x: 2, y: 2, z: 4, core: 2. Of those that a mesh axis runs over, the one named last changes fastest.
Arguments:
- features: float32 [32, 16384], P(None, ('gx', 'gy', 'gz')), may hold values from -6 to 6
- edge_lists: int32 [2, 65536], P(None, ('gx', 'gy', 'gz')), may hold values from 0 to 512, as said below
- peer_nodes: int32 [27, 1024], P(None, ('gx', 'gy', 'gz')), may hold values from 0 to 512, as said below
- edge_in: float32 [2, 32, 64], replicated, may hold values from -0.75 to 0.75
- edge_out: float32 [2, 32, 32], replicated, may hold values from -1 to 1
- node_in: float32 [2, 32, 64], replicated, may hold values from -0.75 to 0.75
- node_out: float32 [2, 32, 32], replicated, may hold values from -1 to 1
- cotangent: float32 [32, 16384], P(None, ('gx', 'gy', 'gz')), may hold values from -6 to 6
Outputs:
- updated: float32 [32, 16384], P(None, ('gx', 'gy', 'gz'))
- feature_grad: float32 [32, 16384], P(None, ('gx', 'gy', 'gz'))
The draws below stay inside these ranges and needn't reach their ends.
Inputs may be any that keep to these rules, and one draw needn't show every extreme that they name: `edge_lists`: row 0 holds sources and row 1 targets. 512 marks an empty edge in both rows; each device's live edges come first, from two fifths of its 2048 slots to all of them, and some device has all live. `peer_nodes`: row k of a device's block lists its nodes coincident with nodes of the device at grid offset (k // 9 - 1, k // 3 % 3 - 1, k % 3 - 1); 512 marks an empty slot and filled slots come first. Slot s of row k and slot s of that neighbour's row 26 - k are filled together and name the same coincident node. No index repeats within a device's block. Row 13 and rows toward devices outside the grid are empty. Rows toward face neighbours fill 32 // 4 to 32 slots, and some pair fills 32; rows toward edge and corner neighbours fill at most 4 slots, and some pair fills 4.
All inputs are finite; a program needn't handle non-finite values.
Results may differ from the reference program's by a relative error of at most 0.0001.
Values sent between devices are 32-bit elements; how exact they have to be, the bound alone decides.
No kernel may reach another device: no remote copies, remote signals or barrier semaphores. Data moves between devices by JAX's collectives and lax.ppermute only.
A program may use at most 64 MiB of HBM per device.

```python
from functools import partial
import jax
import jax.numpy as jnp
import numpy as np
from jax import lax

F = 32
LAYERS = 2
NODES = 512
EDGES = 2048
SLOT = 32
RIM = 4
ALL_NODES = 16384
N_GX = 4
N_GY = 4
N_GZ = 2


def link_offsets():
    return [(link_index // 9 - 1, link_index // 3 % 3 - 1, link_index % 3 - 1) for link_index in range(27)]


def forced_link(select_key, candidates, grid_shape):
    offsets = jnp.asarray(np.array(link_offsets(), dtype=np.int32))
    pick_key, place_key = jax.random.split(select_key)
    table = jnp.asarray(np.array(candidates, dtype=np.int32))
    chosen = table[jax.random.randint(pick_key, (), 0, len(candidates))]
    offset = offsets[chosen]
    lowest = jnp.maximum(-offset, 0)
    highest = jnp.asarray(np.array(grid_shape, dtype=np.int32)) - jnp.maximum(offset, 0)
    place = jax.random.randint(place_key, (3,), lowest, highest)
    return (chosen, place)


def draw_peer_nodes(key, part):
    grid_shape = (N_GX, N_GY, N_GZ)
    device_count = N_GX * N_GY * N_GZ
    base_key = jax.random.fold_in(key, 7)
    face_key, rim_key, first_key, second_key, order_key = jax.random.split(base_key, 5)
    offsets = link_offsets()
    classes = np.array([sum((1 for component in offset if component != 0)) for offset in offsets])
    face_counts = jax.random.randint(face_key, grid_shape + (27,), SLOT // 4, SLOT + 1)
    rim_counts = jax.random.randint(rim_key, grid_shape + (27,), 0, RIM + 1)
    counts = jnp.where(jnp.asarray(classes == 1), face_counts, rim_counts).astype(jnp.int32)
    face_links = [link_index for link_index in range(14, 27) if classes[link_index] == 1]
    rim_links = [link_index for link_index in range(14, 27) if classes[link_index] > 1]
    face_link, face_place = forced_link(first_key, face_links, grid_shape)
    rim_link, rim_place = forced_link(second_key, rim_links, grid_shape)
    counts = counts.at[face_place[0], face_place[1], face_place[2], face_link].set(SLOT)
    counts = counts.at[rim_place[0], rim_place[1], rim_place[2], rim_link].set(RIM)
    coords = [lax.broadcasted_iota(jnp.int32, grid_shape, axis_index) for axis_index in range(3)]
    padded_counts = jnp.pad(counts, ((1, 1), (1, 1), (1, 1), (0, 0)))
    columns = []
    for link_index, offset in enumerate(offsets):
        if link_index > 13:
            inside = jnp.ones(grid_shape, jnp.bool_)
            for axis_index in range(3):
                moved = coords[axis_index] + offset[axis_index]
                inside = inside & (moved >= 0) & (moved < grid_shape[axis_index])
            columns.append(jnp.where(inside, counts[..., link_index], 0))
        elif link_index == 13:
            columns.append(jnp.zeros(grid_shape, jnp.int32))
        else:
            columns.append(padded_counts[1 + offset[0]:1 + offset[0] + N_GX, 1 + offset[1]:1 + offset[1] + N_GY, 1 + offset[2]:1 + offset[2] + N_GZ, 26 - link_index])
    counts_all = jnp.stack(columns, axis=-1).reshape(device_count, 27)
    starts = []
    spans = []
    position = 0
    for link_index in range(27):
        if link_index == 13:
            span = 0
        elif classes[link_index] == 1:
            span = SLOT
        else:
            span = RIM
        starts.append(position)
        spans.append(max(span, 1))
        position = position + span
    start_table = jnp.asarray(np.array(starts, dtype=np.int32))[:, None]
    span_table = jnp.asarray(np.array(spans, dtype=np.int32))[:, None]
    slot_row = lax.broadcasted_iota(jnp.int32, (27, SLOT), 1)
    pick_index = start_table + jnp.minimum(slot_row, span_table - 1)
    order_keys = jax.random.split(order_key, device_count)
    orders = jax.vmap(lambda one_key: jax.random.permutation(one_key, NODES))(order_keys).astype(jnp.int32)
    chosen = jnp.take(orders, pick_index.reshape(-1), axis=1).reshape(device_count, 27, SLOT)
    slot_index = lax.broadcasted_iota(jnp.int32, (device_count, 27, SLOT), 2)
    lists = jnp.where(slot_index < counts_all[:, :, None], chosen, NODES)
    return lists.transpose(1, 0, 2).reshape(27, device_count * SLOT).astype(jnp.int32)


def draw_edge_lists(key, part):
    device_count = N_GX * N_GY * N_GZ
    base_key = jax.random.fold_in(key, 11)
    live_key, pick_key, source_key, stride_key = jax.random.split(base_key, 4)
    live = jax.random.randint(live_key, (device_count,), 2 * EDGES // 5, EDGES + 1)
    full_device = jax.random.randint(pick_key, (), 0, device_count)
    live = jnp.where(lax.broadcasted_iota(jnp.int32, (device_count,), 0) == full_device, EDGES, live)
    sources = jax.random.randint(source_key, (device_count, EDGES), 0, NODES)
    strides = jax.random.randint(stride_key, (device_count, EDGES), 1, 33)
    targets = (sources + strides) % NODES
    slot_index = lax.broadcasted_iota(jnp.int32, (device_count, EDGES), 1)
    used = slot_index < live[:, None]
    sources = jnp.where(used, sources, NODES)
    targets = jnp.where(used, targets, NODES)
    return jnp.stack([sources, targets]).reshape(2, device_count * EDGES).astype(jnp.int32)


def levels(rng, shape, cuts, low, top_value):
    factor_of = 1.0
    for axis_at, parts in cuts:
        steps = jax.random.uniform(jax.random.fold_in(jax.random.fold_in(rng, 6), axis_at), (parts,), jnp.float32, low / len(cuts), top_value / len(cuts))
        factor_of = factor_of * jnp.repeat(jnp.exp(steps), shape[axis_at] // parts).reshape((-1,) + (1,) * (len(shape) - 1 - axis_at))
    return factor_of


def normal_values(stream_key, dims, scale, bound, pieces=(), kind=jnp.bfloat16):
    level = levels(stream_key, dims, pieces, -0.22, 0.18) if pieces else 1.0
    drawn = jax.random.normal(stream_key, dims, jnp.float32) * scale * level
    return jnp.minimum(jnp.maximum(drawn, -bound), bound).astype(kind)


def setup_inputs(seed: int = 0) -> dict:
    splits = jax.random.split(jax.random.key(seed), 9)
    return {
        "features": normal_values(splits[0], (F, ALL_NODES), 1.0, 6.0, ((1, 32),), jnp.float32),
        "edge_lists": draw_edge_lists(jax.random.fold_in(splits[8], 71), 0),
        "peer_nodes": draw_peer_nodes(jax.random.fold_in(splits[8], 71), 0),
        "edge_in": normal_values(splits[3], (LAYERS, F, 2 * F), (2 * F) ** -0.5, 0.75, (), jnp.float32),
        "edge_out": normal_values(splits[4], (LAYERS, F, F), F ** -0.5, 1.0, (), jnp.float32),
        "node_in": normal_values(splits[5], (LAYERS, F, 2 * F), (2 * F) ** -0.5, 0.75, (), jnp.float32),
        "node_out": normal_values(splits[6], (LAYERS, F, F), F ** -0.5, 1.0, (), jnp.float32),
        "cotangent": normal_values(splits[7], (F, ALL_NODES), 1.0, 6.0, ((1, 32),), jnp.float32),
    }


def link_table():
    return [(link_index // 9 - 1, link_index // 3 % 3 - 1, link_index % 3 - 1) for link_index in range(27)]

def with_zero(columns):
    return jnp.concatenate([columns, jnp.zeros(columns.shape[:-1] + (1,), columns.dtype)], axis=-1)

def matmul(left, right):
    return jnp.dot(left, right, precision=lax.Precision.HIGHEST)

def local_partial(field, sources, targets, edge_first, edge_second):
    width = field.shape[0]
    extended = with_zero(field)
    from_source = jnp.take(extended, sources, axis=1)
    from_target = jnp.take(extended, targets, axis=1)
    edge_pre = matmul(edge_first[:, :width], from_source) + matmul(edge_first[:, width:], from_target)
    messages = matmul(edge_second, jax.nn.silu(edge_pre))
    return jnp.zeros_like(extended).at[:, targets].add(messages)[:, :-1]

def take_lists(node_rows, link_lists):
    return jnp.take(node_rows, link_lists, axis=1)

def add_lists(node_rows, link_lists, arrivals):
    return node_rows.at[:, link_lists.reshape(-1)].add(arrivals)

def assemble_all(partials, lists):
    device_count = partials.shape[0]
    width = partials.shape[1]
    slots = lists.shape[2]
    extended = with_zero(partials)
    outgoing = jax.vmap(take_lists)(extended, lists)
    grid = outgoing.reshape(N_GX, N_GY, N_GZ, width, 27, slots)
    border = jnp.pad(grid, ((1, 1), (1, 1), (1, 1), (0, 0), (0, 0), (0, 0)))
    incoming = []
    for link_index, offset in enumerate(link_table()):
        incoming.append(border[1 + offset[0]:1 + offset[0] + N_GX, 1 + offset[1]:1 + offset[1] + N_GY, 1 + offset[2]:1 + offset[2] + N_GZ, :, 26 - link_index])
    incoming = jnp.stack(incoming, axis=4).reshape(device_count, width, 27 * slots)
    summed = jax.vmap(add_lists)(extended, lists, incoming)
    return summed[:, :, :-1]

def forward(features, edge_lists, peer_nodes, edge_in, edge_out, node_in, node_out):
    width = features.shape[0]
    device_count = N_GX * N_GY * N_GZ
    field = features.reshape(width, device_count, NODES).transpose(1, 0, 2)
    sources = edge_lists[0].reshape(device_count, EDGES)
    targets = edge_lists[1].reshape(device_count, EDGES)
    lists = peer_nodes.reshape(27, device_count, SLOT).transpose(1, 0, 2)
    for layer_index in range(LAYERS):
        edge_first = edge_in[layer_index]
        edge_second = edge_out[layer_index]

        def partial_of(items):
            return local_partial(items[0], items[1], items[2], edge_first, edge_second)
        partials = lax.map(partial_of, (field, sources, targets))
        aggregate = assemble_all(partials, lists)
        node_first = node_in[layer_index]
        node_pre = jnp.einsum('of,dfn->don', node_first[:, :width], field, precision=lax.Precision.HIGHEST)
        node_pre = node_pre + jnp.einsum('of,dfn->don', node_first[:, width:], aggregate, precision=lax.Precision.HIGHEST)
        field = field + jnp.einsum('of,dfn->don', node_out[layer_index], jax.nn.silu(node_pre), precision=lax.Precision.HIGHEST)
    return field.transpose(1, 0, 2).reshape(width, device_count * NODES)

def reference(features, edge_lists, peer_nodes, edge_in, edge_out, node_in, node_out, cotangent):
    closed = partial(forward, edge_lists=edge_lists, peer_nodes=peer_nodes, edge_in=edge_in, edge_out=edge_out, node_in=node_in, node_out=node_out)
    updated, pullback = jax.vjp(closed, features)
    feature_grad = pullback(cotangent)[0]
    return (updated, feature_grad)
```

```python
import functools

import jax
import jax.numpy as jnp
from jax import lax
from jax.experimental import pallas as pl
from jax.experimental.pallas import tpu as pltpu
from jax.sharding import PartitionSpec as P

AXES = ("gx", "gy", "gz")
LANES = 128
FACES = (4, 22, 10, 16, 12, 14)
RIMS = tuple(
    link for low in (0, 1, 2, 3, 5, 6, 7, 8, 9, 11) for link in (low, 26 - low)
)
BF16 = jnp.bfloat16
F32 = jnp.float32


def pieces(values):
    high = values.astype(BF16)
    low = (values - high.astype(F32)).astype(BF16)
    return high, low


def stacked(values):
    return jnp.concatenate(pieces(values), axis=0)


def folded(values):
    half = values.shape[0] // 2
    return values[:half] + values[half:]


def dot(left, right):
    return jnp.dot(left, right, preferred_element_type=F32)


def dot_rows(left, right):
    return lax.dot_general(
        left, right, (((1,), (1,)), ((), ())), preferred_element_type=F32
    )


def weigh(weight, values):
    high, low = pieces(values)
    rows = weight.shape[0]
    both = stacked(weight)
    first = dot(both, high)
    return first[:rows] + (first[rows:] + dot(both[:rows], low))


def gather(values, one_hot):
    return folded(dot(stacked(values), one_hot))


def scatter(values, one_hot):
    return folded(dot_rows(stacked(values), one_hot))


def sigmoid(values):
    return 0.5 * jnp.tanh(0.5 * values) + 0.5


def silu(values):
    return values * sigmoid(values)


def silu_slope(values):
    gate = sigmoid(values)
    return gate * (1.0 + values * (1.0 - gate))


class Layout:
    def __init__(self, width, slots, counts):
        self.width = width
        self.slots = slots
        self.rim = max(slots // 8, 2)
        self.per_group = slots // self.rim
        self.parts = LANES // slots
        self.rows = width // self.parts
        groups = -(-len(RIMS) // self.per_group)
        self.bands = len(FACES) + groups
        self.columns = -(-self.bands // self.parts)
        self.lanes = self.columns * LANES
        self.counts = counts
        self.devices = counts[0] * counts[1] * counts[2]

    def band_of(self, link):
        if link in FACES:
            return FACES.index(link)
        return len(FACES) + RIMS.index(link) // self.per_group

    def neighbours(self):
        place = [lax.axis_index(axis) for axis in AXES]
        nx, ny, nz = self.counts
        mine = (place[0] * ny + place[1]) * nz + place[2]
        table = {}
        for link in FACES + RIMS:
            moved = [
                place[0] + (link // 9 - 1),
                place[1] + (link // 3 % 3 - 1),
                place[2] + (link % 3 - 1),
            ]
            inside = None
            for at, count in zip(moved, self.counts):
                here = jnp.logical_and(at >= 0, at < count)
                inside = here if inside is None else jnp.logical_and(inside, here)
            there = (moved[0] * ny + moved[1]) * nz + moved[2]
            table[link] = jnp.where(inside, there, mine)
        return table


def slot_row(layout, peer):
    empty = 1 << 20
    pieces_of = [peer[link : link + 1, : layout.slots] for link in FACES]
    pieces_of += [peer[link : link + 1, : layout.rim] for link in RIMS]
    used = len(FACES) * layout.slots + len(RIMS) * layout.rim
    pieces_of.append(jnp.full((1, layout.lanes - used), empty, jnp.int32))
    return jnp.concatenate(pieces_of, axis=1)


def swap_parts(layout, blocks):
    parts = layout.parts
    rows = blocks[0].shape[0]
    part = lax.broadcasted_iota(jnp.int32, (rows, LANES), 1) // layout.slots
    result = []
    for band in range(parts):
        tile = None
        for group in range(parts):
            shift = (layout.slots * (group - band)) % LANES
            moved = blocks[group]
            if shift:
                moved = pltpu.roll(moved, shift, 1)
            tile = moved if tile is None else jnp.where(part == group, moved, tile)
        result.append(tile)
    return result


def send(layout, table, values, send_ref, at):
    tiles = []
    for column in range(layout.columns):
        lanes = slice(column * LANES, (column + 1) * LANES)
        blocks = [
            values[group * layout.rows : (group + 1) * layout.rows, lanes]
            for group in range(layout.parts)
        ]
        tiles += swap_parts(layout, blocks)
    for link in FACES + RIMS:
        send_ref[table[link], at * layout.rows : (at + 1) * layout.rows, :] = tiles[
            layout.band_of(link)
        ]


def receive(layout, table, got_ref, at):
    rows = slice(at * layout.rows, (at + 1) * layout.rows)
    lane = lax.broadcasted_iota(jnp.int32, (layout.rows, LANES), 1)
    place = lane % layout.slots // layout.rim
    tiles = [got_ref[table[link], rows, :] for link in FACES]
    for start in range(0, len(RIMS), layout.per_group):
        tile = None
        for index, link in enumerate(RIMS[start : start + layout.per_group]):
            block = got_ref[table[link], rows, :]
            tile = block if tile is None else jnp.where(place == index ^ 1, block, tile)
        up = pltpu.roll(tile, layout.rim, 1)
        down = pltpu.roll(tile, LANES - layout.rim, 1)
        tiles.append(jnp.where(place % 2 == 1, up, down))
    while len(tiles) < layout.columns * layout.parts:
        tiles.append(jnp.zeros((layout.rows, LANES), F32))
    columns = []
    for column in range(layout.columns):
        blocks = swap_parts(layout, tiles[column * layout.parts : (column + 1) * layout.parts])
        columns.append(jnp.concatenate(blocks, axis=0))
    return jnp.concatenate(columns, axis=1)


def one_hot(indices, count):
    rows = lax.broadcasted_iota(jnp.int32, (count, indices.shape[1]), 0)
    return jnp.where(rows == indices, 1.0, 0.0).astype(BF16)


CHUNK = 512


def edges_forward(field, first, second, hot_ref, pre_ref):
    width, nodes = field.shape
    both = weigh(jnp.concatenate([first[:, :width], first[:, width:]], axis=0), field)
    ends = jnp.concatenate([stacked(both[:width]), stacked(both[width:])], axis=1)
    total = None
    for start in range(0, hot_ref.shape[1], CHUNK):
        span = slice(start, start + CHUNK)
        pre = folded(dot(ends, hot_ref[:, span]))
        pre_ref[:, span] = pre
        term = dot_rows(stacked(silu(pre)), hot_ref[nodes:, span])
        total = term if total is None else total + term
    return weigh(second, folded(total))


def edges_backward(partial_grad, first, second, hot_ref, pre_ref):
    width, nodes = partial_grad.shape
    pulled = stacked(weigh(second.T, partial_grad))
    total = None
    for start in range(0, hot_ref.shape[1], CHUNK):
        span = slice(start, start + CHUNK)
        delta = folded(dot(pulled, hot_ref[nodes:, span])) * silu_slope(pre_ref[:, span])
        term = dot_rows(stacked(delta), hot_ref[:, span])
        total = term if total is None else total + term
    total = folded(total)
    return weigh(first[:, :width].T, total[:, :nodes]) + weigh(
        first[:, width:].T, total[:, nodes:]
    )


def first_kernel(
    layout, field_ref, edges_ref, peer_ref, first_ref, second_ref,
    hot_ref, slot_hot_ref, pre_ref, partial_ref, send_ref,
):
    nodes = field_ref.shape[1]
    table = layout.neighbours()
    for start in range(0, edges_ref.shape[1], CHUNK):
        span = slice(start, start + CHUNK)
        hot_ref[:nodes, span] = one_hot(edges_ref[0:1, span], nodes)
        hot_ref[nodes:, span] = one_hot(edges_ref[1:2, span], nodes)
    slot_hot_ref[...] = one_hot(slot_row(layout, peer_ref[...]), nodes)
    partial = edges_forward(field_ref[...], first_ref[0], second_ref[0], hot_ref, pre_ref)
    partial_ref[...] = partial
    send(layout, table, gather(partial, slot_hot_ref[...]), send_ref, 0)


def second_kernel(
    layout, got_ref, partial_ref, field_ref, cotangent_ref, hot_ref, slot_hot_ref,
    first_ref, second_ref, node_in_ref, node_out_ref,
    node_pre_ref, next_ref, pre_ref, next_partial_ref, ghost_ref, send_ref,
):
    width = field_ref.shape[0]
    table = layout.neighbours()
    slot_hot = slot_hot_ref[...]
    aggregate = partial_ref[...] + scatter(receive(layout, table, got_ref, 0), slot_hot)
    field = field_ref[...]
    node_pre = weigh(node_in_ref[0], jnp.concatenate([field, aggregate], axis=0))
    node_pre_ref[...] = node_pre
    field = field + weigh(node_out_ref[0], silu(node_pre))
    next_ref[...] = field
    partial = edges_forward(field, first_ref[1], second_ref[1], hot_ref, pre_ref)
    next_partial_ref[...] = partial
    own = weigh(node_in_ref[1, :, :width], field)
    pulled = weigh(node_out_ref[1].T, cotangent_ref[...])
    ghost_ref[0] = own
    ghost_ref[1] = pulled
    send(layout, table, gather(partial, slot_hot), send_ref, 0)
    send(layout, table, gather(own, slot_hot), send_ref, 1)
    send(layout, table, gather(pulled, slot_hot), send_ref, 2)


def third_kernel(
    layout, got_ref, partial_ref, field_ref, cotangent_ref, ghost_ref, pre_ref, node_pre_ref,
    hot_ref, slot_hot_ref, first_ref, second_ref, node_in_ref, node_out_ref,
    updated_ref, field_grad_ref, aggregate_grad_ref, send_ref,
):
    width = field_ref.shape[0]
    table = layout.neighbours()
    slot_hot = slot_hot_ref[...]
    arrived = receive(layout, table, got_ref, 0)
    aggregate = partial_ref[...] + scatter(arrived, slot_hot)
    from_aggregate = weigh(node_in_ref[1, :, width:], aggregate)
    node_pre = ghost_ref[0] + from_aggregate
    updated_ref[...] = field_ref[...] + weigh(node_out_ref[1], silu(node_pre))
    delta = ghost_ref[1] * silu_slope(node_pre)
    peer_pre = receive(layout, table, got_ref, 1) + gather(from_aggregate, slot_hot)
    peer_delta = receive(layout, table, got_ref, 2) * silu_slope(peer_pre)
    pulled = weigh(node_in_ref[1].T, delta)
    partial_grad = pulled[width:] + weigh(
        node_in_ref[1, :, width:].T, scatter(peer_delta, slot_hot)
    )
    upstream = cotangent_ref[...] + pulled[:width]
    upstream = upstream + edges_backward(
        partial_grad, first_ref[1], second_ref[1], hot_ref, pre_ref
    )
    delta = weigh(node_out_ref[0].T, upstream) * silu_slope(node_pre_ref[...])
    pulled = weigh(node_in_ref[0].T, delta)
    field_grad_ref[...] = upstream + pulled[:width]
    aggregate_grad_ref[...] = pulled[width:]
    send(layout, table, gather(pulled[width:], slot_hot), send_ref, 0)


def fourth_kernel(
    layout, got_ref, aggregate_grad_ref, field_grad_ref, pre_ref, hot_ref, slot_hot_ref,
    first_ref, second_ref, grad_ref,
):
    table = layout.neighbours()
    arrived = receive(layout, table, got_ref, 0)
    partial_grad = aggregate_grad_ref[...] + scatter(arrived, slot_hot_ref[...])
    grad_ref[...] = field_grad_ref[...] + edges_backward(
        partial_grad, first_ref[0], second_ref[0], hot_ref, pre_ref
    )


def call(kernel, layout, shapes, *arrays):
    return pl.pallas_call(
        functools.partial(kernel, layout),
        out_shape=[jax.ShapeDtypeStruct(shape, kind) for shape, kind in shapes],
        in_specs=[pl.BlockSpec(memory_space=pltpu.VMEM)] * len(arrays),
        out_specs=[pl.BlockSpec(memory_space=pltpu.VMEM)] * len(shapes),
        compiler_params=pltpu.CompilerParams(vmem_limit_bytes=40 << 20),
    )(*arrays)


def exchanged(blocks):
    return lax.all_to_all(blocks, AXES, 0, 0)


def on_device(counts, features, edge_lists, peer_nodes, edge_in, edge_out, node_in, node_out, cotangent):
    width, nodes = features.shape
    edges = edge_lists.shape[1]
    layout = Layout(width, peer_nodes.shape[1], counts)
    rows, devices = layout.rows, layout.devices
    field_like = ((width, nodes), F32)
    edge_like = ((width, edges), F32)
    hot, slot_hot, pre_1, partial_1, blocks = call(
        first_kernel, layout,
        [((2 * nodes, edges), BF16), ((nodes, layout.lanes), BF16), edge_like, field_like,
         ((devices, rows, LANES), F32)],
        features, edge_lists, peer_nodes, edge_in, edge_out,
    )
    got = exchanged(blocks)
    node_pre_1, field_2, pre_2, partial_2, ghost, blocks = call(
        second_kernel, layout,
        [field_like, field_like, edge_like, field_like, ((2, width, nodes), F32),
         ((devices, 3 * rows, LANES), F32)],
        got, partial_1, features, cotangent, hot, slot_hot, edge_in, edge_out, node_in, node_out,
    )
    got = exchanged(blocks)
    updated, field_grad, aggregate_grad, blocks = call(
        third_kernel, layout,
        [field_like, field_like, field_like, ((devices, rows, LANES), F32)],
        got, partial_2, field_2, cotangent, ghost, pre_2, node_pre_1, hot, slot_hot,
        edge_in, edge_out, node_in, node_out,
    )
    got = exchanged(blocks)
    (feature_grad,) = call(
        fourth_kernel, layout, [field_like],
        got, aggregate_grad, field_grad, pre_1, hot, slot_hot, edge_in, edge_out,
    )
    return updated, feature_grad


def solution(mesh):
    split = P(None, AXES)
    counts = tuple(mesh.shape[axis] for axis in AXES)
    return jax.shard_map(
        functools.partial(on_device, counts),
        mesh=mesh,
        in_specs=(split, split, split, P(), P(), P(), P(), split),
        out_specs=(split, split),
        check_vma=False,
    )
```

```python
import functools

import jax
import jax.numpy as jnp
from jax import lax
from jax.experimental import pallas as pl
from jax.experimental.pallas import tpu as pltpu
from jax.sharding import PartitionSpec as P

AXES = ("gx", "gy", "gz")
LANES = 128
FACES = (4, 22, 10, 16, 12, 14)
RIMS = tuple(
    link for low in (0, 1, 2, 3, 5, 6, 7, 8, 9, 11) for link in (low, 26 - low)
)
BLOCK = 256
CHUNK = 512
BF16 = jnp.bfloat16
F32 = jnp.float32


class Layout:
    def __init__(self, width, slots, counts):
        self.width = width
        self.slots = slots
        self.rim = max(slots // 8, 2)
        self.per_group = slots // self.rim
        self.parts = LANES // slots
        self.rows = width // self.parts
        groups = -(-len(RIMS) // self.per_group)
        self.bands = len(FACES) + groups
        self.columns = -(-self.bands // self.parts)
        self.lanes = self.columns * LANES
        self.counts = counts
        self.devices = counts[0] * counts[1] * counts[2]

    def band_of(self, link):
        if link in FACES:
            return FACES.index(link)
        return len(FACES) + RIMS.index(link) // self.per_group

    def neighbours(self):
        place = [lax.axis_index(axis) for axis in AXES]
        nx, ny, nz = self.counts
        mine = (place[0] * ny + place[1]) * nz + place[2]
        table = {}
        for link in FACES + RIMS:
            moved = [
                place[0] + (link // 9 - 1),
                place[1] + (link // 3 % 3 - 1),
                place[2] + (link % 3 - 1),
            ]
            inside = None
            for at, count in zip(moved, self.counts):
                here = jnp.logical_and(at >= 0, at < count)
                inside = here if inside is None else jnp.logical_and(inside, here)
            there = (moved[0] * ny + moved[1]) * nz + moved[2]
            table[link] = jnp.where(inside, there, mine)
        return table


def slot_row(layout, peer):
    empty = 1 << 20
    pieces_of = [peer[link : link + 1, : layout.slots] for link in FACES]
    pieces_of += [peer[link : link + 1, : layout.rim] for link in RIMS]
    used = len(FACES) * layout.slots + len(RIMS) * layout.rim
    pieces_of.append(jnp.full((1, layout.lanes - used), empty, jnp.int32))
    return jnp.concatenate(pieces_of, axis=1)


def swap_parts(layout, blocks):
    parts = layout.parts
    rows = blocks[0].shape[0]
    part = lax.broadcasted_iota(jnp.int32, (rows, LANES), 1) // layout.slots
    result = []
    for band in range(parts):
        tile = None
        for group in range(parts):
            shift = (layout.slots * (group - band)) % LANES
            moved = blocks[group]
            if shift:
                moved = pltpu.roll(moved, shift, 1)
            tile = moved if tile is None else jnp.where(part == group, moved, tile)
        result.append(tile)
    return result


def send(layout, table, values, send_ref, at):
    tiles = []
    for column in range(layout.columns):
        lanes = slice(column * LANES, (column + 1) * LANES)
        blocks = [
            values[group * layout.rows : (group + 1) * layout.rows, lanes]
            for group in range(layout.parts)
        ]
        tiles += swap_parts(layout, blocks)
    for link in FACES + RIMS:
        send_ref[table[link], at * layout.rows : (at + 1) * layout.rows, :] = tiles[
            layout.band_of(link)
        ]


def receive(layout, table, got_ref, at):
    rows = slice(at * layout.rows, (at + 1) * layout.rows)
    lane = lax.broadcasted_iota(jnp.int32, (layout.rows, LANES), 1)
    place = lane % layout.slots // layout.rim
    tiles = [got_ref[table[link], rows, :] for link in FACES]
    for start in range(0, len(RIMS), layout.per_group):
        tile = None
        for index, link in enumerate(RIMS[start : start + layout.per_group]):
            block = got_ref[table[link], rows, :]
            tile = block if tile is None else jnp.where(place == index ^ 1, block, tile)
        up = pltpu.roll(tile, layout.rim, 1)
        down = pltpu.roll(tile, LANES - layout.rim, 1)
        tiles.append(jnp.where(place % 2 == 1, up, down))
    while len(tiles) < layout.columns * layout.parts:
        tiles.append(jnp.zeros((layout.rows, LANES), F32))
    columns = []
    for column in range(layout.columns):
        blocks = swap_parts(layout, tiles[column * layout.parts : (column + 1) * layout.parts])
        columns.append(jnp.concatenate(blocks, axis=0))
    return jnp.concatenate(columns, axis=1)


def pieces(values):
    high = values.astype(BF16)
    low = (values - high.astype(F32)).astype(BF16)
    return high, low


def dot(left, right):
    return jnp.dot(left, right, preferred_element_type=F32)


def dot_rows(left, right):
    return lax.dot_general(
        left, right, (((1,), (1,)), ((), ())), preferred_element_type=F32
    )


def exact(left, right):
    return jnp.dot(left, right, precision=lax.Precision.HIGHEST, preferred_element_type=F32)


def prepared(weight):
    high = weight.astype(BF16).astype(F32)
    return jnp.concatenate([high, weight - high, high], axis=1).astype(BF16)


def weigh(weight, values):
    high, low = pieces(values)
    return dot(weight, jnp.concatenate([high, high, low], axis=0))


def sigmoid(values):
    return 0.5 * jnp.tanh(0.5 * values) + 0.5


def silu(values):
    return values * sigmoid(values)


def silu_slope(values):
    gate = sigmoid(values)
    return gate * (1.0 + values * (1.0 - gate))


def one_hot(indices):
    places = jnp.where(indices < 0, -1, indices % BLOCK)
    places = jnp.broadcast_to(places, (16, indices.shape[1])).astype(F32).astype(BF16)
    places = jnp.concatenate([places] * (BLOCK // 16), axis=0)
    rows = lax.broadcasted_iota(jnp.int32, (BLOCK, indices.shape[1]), 0)
    rows = rows.astype(F32).astype(BF16)
    return jnp.where(rows == places, jnp.ones((), BF16), jnp.zeros((), BF16))


def gather_rows(values):
    high, low = pieces(values)
    rows = []
    for start in range(0, values.shape[1], BLOCK):
        rows += [high[:, start : start + BLOCK], low[:, start : start + BLOCK]]
    return jnp.concatenate(rows, axis=0)


def pick(found, indices, width):
    result = None
    for block in range(found.shape[0] // (2 * width)):
        at = 2 * width * block
        value = found[at : at + width] + found[at + width : at + 2 * width]
        result = value if result is None else jnp.where(indices >= block * BLOCK, value, result)
    return result


def gather(values, hot, indices):
    return pick(dot(gather_rows(values), hot), indices, values.shape[0])


def block_rows(values, indices, blocks):
    high, low = pieces(values)
    rows = []
    for block in range(blocks):
        inside = jnp.logical_and(indices >= block * BLOCK, indices < (block + 1) * BLOCK)
        mask = jnp.broadcast_to(jnp.where(inside, 1.0, 0.0), (16, indices.shape[1])).astype(BF16)
        mask = jnp.concatenate([mask] * (values.shape[0] // 16), axis=0)
        rows += [high * mask, low * mask]
    return jnp.concatenate(rows, axis=0)


def unblocked(summed, width):
    columns = []
    for at in range(0, summed.shape[0], 2 * width):
        columns.append(summed[at : at + width] + summed[at + width : at + 2 * width])
    return jnp.concatenate(columns, axis=1)


def scatter(values, hot, indices, blocks):
    return unblocked(dot_rows(block_rows(values, indices, blocks), hot), values.shape[0])


def add(total, term):
    return term if total is None else total + term


def edges_forward(ends, edges_ref, hot_ref, pre_ref):
    width, nodes = ends.shape[0] // 2, ends.shape[1]
    left = gather_rows(ends[:width]), gather_rows(ends[width:])
    total = None
    for start in range(0, edges_ref.shape[1], CHUNK):
        span = slice(start, start + CHUNK)
        pre = None
        for side in range(2):
            found = dot(left[side], hot_ref[side, :, span])
            pre = add(pre, pick(found, edges_ref[side : side + 1, span], width))
        pre_ref[:, span] = pre
        rows = block_rows(silu(pre), edges_ref[1:2, span], nodes // BLOCK)
        total = add(total, dot_rows(rows, hot_ref[1, :, span]))
    return unblocked(total, width)


def edges_backward(pulled, edges_ref, hot_ref, pre_ref):
    width, nodes = pulled.shape
    left = gather_rows(pulled)
    totals = [None, None]
    for start in range(0, edges_ref.shape[1], CHUNK):
        span = slice(start, start + CHUNK)
        found = dot(left, hot_ref[1, :, span])
        delta = pick(found, edges_ref[1:2, span], width) * silu_slope(pre_ref[:, span])
        for side in range(2):
            rows = block_rows(delta, edges_ref[side : side + 1, span], nodes // BLOCK)
            totals[side] = add(totals[side], dot_rows(rows, hot_ref[side, :, span]))
    return jnp.concatenate([unblocked(total, width) for total in totals], axis=0)


def first_kernel(
    layout, opened_ref, features_ref, lists_ref, peer_ref, edge_in_ref, edge_out_ref,
    node_in_ref, node_out_ref, grad_ref,
    field_ref, cotangent_ref, edges_ref, hot_ref, slots_ref, slot_hot_ref, base_ref, pulled_ref,
    pre_ref, joined_ref, send_ref,
    weight_1_ref, weight_2_ref, weight_3_ref, weight_4_ref, weight_5_ref, weight_6_ref,
    weight_7_ref, weight_8_ref,
):
    table = layout.neighbours()
    width, nodes = field_ref.shape
    field_ref[...] = features_ref[...]
    cotangent_ref[...] = grad_ref[...]
    edges_ref[...] = lists_ref[...]
    for side in range(2):
        for start in range(0, edges_ref.shape[1], CHUNK):
            span = slice(start, start + CHUNK)
            indices = lists_ref[side : side + 1, span]
            hot_ref[side, :, span] = one_hot(jnp.where(indices < nodes, indices, -1))
    slots = slot_row(layout, peer_ref[...])
    slots = jnp.where(slots < nodes, slots, -1)
    slots_ref[...] = jnp.broadcast_to(slots, slots_ref.shape)
    slot_hot_ref[...] = one_hot(slots)
    edge_1, edge_2 = edge_in_ref[0], edge_in_ref[1]
    node_1, node_2 = node_in_ref[0], node_in_ref[1]
    out_1, out_2 = node_out_ref[0], node_out_ref[1]
    ends_1 = jnp.concatenate([edge_1[:, :width], edge_1[:, width:]], axis=0)
    after = jnp.concatenate([edge_2[:, :width], edge_2[:, width:], node_2[:, :width]], axis=0)
    from_field = prepared(jnp.concatenate([ends_1, node_1[:, :width], after], axis=0))
    moved = weigh(from_field, features_ref[...])
    base_ref[...] = moved[2 * width :]
    join_1 = exact(node_1[:, width:], edge_out_ref[0])
    summed = edges_forward(moved[: 2 * width], lists_ref, hot_ref, pre_ref)
    joined = weigh(prepared(join_1), summed)
    joined_ref[...] = joined
    send(layout, table, gather(joined, slot_hot_ref[...], slots), send_ref, 0)
    join_2 = exact(node_2[:, width:], edge_out_ref[1])
    after_out = exact(after, out_1)
    weight_1_ref[...] = prepared(jnp.concatenate([out_1, after_out], axis=0))
    weight_2_ref[...] = prepared(join_2)
    weight_3_ref[...] = prepared(out_2)
    weight_4_ref[...] = prepared(join_2.T)
    back = jnp.concatenate(
        [jnp.concatenate([after, after_out], axis=1), jnp.zeros((width, 2 * width), F32)], axis=0
    ).T
    weight_5_ref[...] = prepared(back[:, : 2 * width])
    weight_6_ref[...] = prepared(back[:, 2 * width : 3 * width])
    weight_7_ref[...] = prepared(
        jnp.concatenate([join_1.T, node_1[:, :width].T], axis=0)
    )
    weight_8_ref[...] = prepared(ends_1.T)
    pulls = prepared(jnp.concatenate([out_1.T, out_2.T], axis=0))
    pulled_ref[...] = weigh(pulls, grad_ref[...])


def second_kernel(
    layout, got_ref, joined_ref, field_ref, base_ref, pulled_ref, edges_ref, hot_ref, slots_ref,
    slot_hot_ref, weight_1_ref, weight_2_ref,
    node_pre_ref, next_ref, own_ref, pre_ref, next_joined_ref, at_slots_ref, send_ref,
):
    width, nodes = field_ref.shape
    table = layout.neighbours()
    slots, slot_hot = slots_ref[0:1], slot_hot_ref[...]
    arrived = receive(layout, table, got_ref, 0)
    joined = joined_ref[...] + scatter(arrived, slot_hot, slots, nodes // BLOCK)
    node_pre = base_ref[:width] + joined
    node_pre_ref[...] = node_pre
    changes = weigh(weight_1_ref[...], silu(node_pre))
    next_ref[...] = field_ref[...] + changes[:width]
    moved = base_ref[width:] + changes[width:]
    own_ref[...] = moved[2 * width :]
    summed = edges_forward(moved[: 2 * width], edges_ref, hot_ref, pre_ref)
    joined = weigh(weight_2_ref[...], summed)
    next_joined_ref[...] = joined
    at_slots = gather(joined, slot_hot, slots)
    at_slots_ref[...] = at_slots
    send(layout, table, at_slots, send_ref, 0)
    send(layout, table, gather(moved[2 * width :], slot_hot, slots), send_ref, 1)
    send(layout, table, gather(pulled_ref[width:], slot_hot, slots), send_ref, 2)


def third_kernel(
    layout, got_ref, joined_ref, at_slots_ref, field_ref, cotangent_ref, own_ref, pulled_ref,
    pre_ref, node_pre_ref, edges_ref, hot_ref, slots_ref, slot_hot_ref,
    weight_3_ref, weight_4_ref, weight_5_ref, weight_6_ref, weight_7_ref,
    updated_ref, field_grad_ref, joined_grad_ref, send_ref,
):
    width, nodes = field_ref.shape
    table = layout.neighbours()
    slots, slot_hot = slots_ref[0:1], slot_hot_ref[...]
    arrived = receive(layout, table, got_ref, 0)
    peer_pre = receive(layout, table, got_ref, 1) + (at_slots_ref[...] + arrived)
    peer_delta = receive(layout, table, got_ref, 2) * silu_slope(peer_pre)
    joined = joined_ref[...] + scatter(arrived, slot_hot, slots, nodes // BLOCK)
    node_pre = own_ref[...] + joined
    updated_ref[...] = field_ref[...] + weigh(weight_3_ref[...], silu(node_pre))
    delta = pulled_ref[width:] * silu_slope(node_pre)
    both = delta + scatter(peer_delta, slot_hot, slots, nodes // BLOCK)
    summed = edges_backward(weigh(weight_4_ref[...], both), edges_ref, hot_ref, pre_ref)
    changes = weigh(weight_5_ref[...], summed) + weigh(weight_6_ref[...], delta)
    upstream = cotangent_ref[...] + changes[:width]
    delta = (pulled_ref[:width] + changes[width:]) * silu_slope(node_pre_ref[...])
    back = weigh(weight_7_ref[...], delta)
    joined_grad_ref[...] = back[:width]
    send(layout, table, gather(back[:width], slot_hot, slots), send_ref, 0)
    field_grad_ref[...] = upstream + back[width:]


def fourth_kernel(
    layout, got_ref, joined_grad_ref, field_grad_ref, pre_ref, edges_ref, hot_ref, slots_ref,
    slot_hot_ref, weight_8_ref, grad_ref,
):
    nodes = joined_grad_ref.shape[1]
    table = layout.neighbours()
    arrived = receive(layout, table, got_ref, 0)
    pulled = joined_grad_ref[...] + scatter(
        arrived, slot_hot_ref[...], slots_ref[0:1], nodes // BLOCK
    )
    summed = edges_backward(pulled, edges_ref, hot_ref, pre_ref)
    grad_ref[...] = field_grad_ref[...] + weigh(weight_8_ref[...], summed)


def opening_kernel(opened_ref):
    opened_ref[...] = jnp.zeros(opened_ref.shape, jnp.int32)


def call(kernel, layout, shapes, arrays):
    return pl.pallas_call(
        functools.partial(kernel, layout),
        out_shape=[jax.ShapeDtypeStruct(shape, kind) for shape, kind in shapes],
        in_specs=[pl.BlockSpec(memory_space=pltpu.VMEM)] * len(arrays),
        out_specs=[pl.BlockSpec(memory_space=pltpu.VMEM)] * len(shapes),
        compiler_params=pltpu.CompilerParams(vmem_limit_bytes=40 << 20),
    )(*arrays)


def exchanged(blocks):
    return lax.all_to_all(blocks, AXES, 0, 0)


def on_device(counts, features, edge_lists, peer_nodes, edge_in, edge_out, node_in, node_out, cotangent):
    width, nodes = features.shape
    edges = edge_lists.shape[1]
    layout = Layout(width, peer_nodes.shape[1], counts)
    rows, devices, lanes = layout.rows, layout.devices, layout.lanes
    like = lambda times: ((times * width, nodes), F32)
    edge_like = ((width, edges), F32)
    weight = lambda tall, wide: ((tall * width, 3 * wide * width), BF16)
    sent = lambda times: ((devices, times * rows, LANES), F32)
    opened = pl.pallas_call(
        opening_kernel,
        out_shape=jax.ShapeDtypeStruct((8, LANES), jnp.int32),
        out_specs=pl.BlockSpec(memory_space=pltpu.VMEM),
        cost_estimate=pl.CostEstimate(flops=10**10, bytes_accessed=10**7, transcendentals=0),
        compiler_params=pltpu.CompilerParams(vmem_limit_bytes=1 << 20),
    )()
    (field, pull, lists, hot, slots, slot_hot, base, pulled, pre_1, joined, blocks,
     *weights) = call(
        first_kernel, layout,
        [like(1), like(1), ((2, edges), jnp.int32), ((2, BLOCK, edges), BF16),
         ((8, lanes), jnp.int32), ((BLOCK, lanes), BF16), like(4), like(2), edge_like, like(1),
         sent(1),
         weight(4, 1), weight(1, 1), weight(1, 1), weight(1, 1), weight(2, 2), weight(2, 1),
         weight(2, 1), weight(1, 2)],
        [opened, features, edge_lists, peer_nodes, edge_in, edge_out, node_in, node_out, cotangent],
    )
    got = exchanged(blocks)
    node_pre, next_field, own, pre_2, joined, at_slots, blocks = call(
        second_kernel, layout,
        [like(1), like(1), like(1), edge_like, like(1), ((width, lanes), F32), sent(3)],
        [got, joined, field, base, pulled, lists, hot, slots, slot_hot, weights[0], weights[1]],
    )
    got = exchanged(blocks)
    updated, field_grad, joined_grad, blocks = call(
        third_kernel, layout,
        [like(1), like(1), like(1), sent(1)],
        [got, joined, at_slots, next_field, pull, own, pulled, pre_2, node_pre, lists, hot, slots,
         slot_hot, *weights[2:7]],
    )
    got = exchanged(blocks)
    (feature_grad,) = call(
        fourth_kernel, layout, [like(1)],
        [got, joined_grad, field_grad, pre_1, lists, hot, slots, slot_hot, weights[7]],
    )
    return updated, feature_grad


def solution(mesh):
    split = P(None, AXES)
    counts = tuple(mesh.shape[axis] for axis in AXES)
    return jax.shard_map(
        functools.partial(on_device, counts),
        mesh=mesh,
        in_specs=(split, split, split, P(), P(), P(), P(), split),
        out_specs=(split, split),
        check_vma=False,
    )
```

```python
import functools

import jax
import jax.numpy as jnp
from jax import lax
from jax.experimental import pallas as pl
from jax.experimental.pallas import tpu as pltpu
from jax.sharding import PartitionSpec as P

AXES = ("gx", "gy", "gz")
LANES = 128
FACES = (4, 22, 10, 16, 12, 14)
RIMS = tuple(
    link for low in (0, 1, 2, 3, 5, 6, 7, 8, 9, 11) for link in (low, 26 - low)
)
BLOCK = 256
CHUNK = 2048
BF16 = jnp.bfloat16
F32 = jnp.float32


class Layout:
    def __init__(self, width, slots, counts):
        self.width = width
        self.slots = slots
        self.rim = max(slots // 8, 2)
        self.per_group = slots // self.rim
        self.parts = LANES // slots
        self.rows = width // self.parts
        groups = -(-len(RIMS) // self.per_group)
        self.bands = len(FACES) + groups
        self.columns = -(-self.bands // self.parts)
        self.lanes = self.columns * LANES
        self.counts = counts
        self.devices = counts[0] * counts[1] * counts[2]

    def band_of(self, link):
        if link in FACES:
            return FACES.index(link)
        return len(FACES) + RIMS.index(link) // self.per_group

    def neighbours(self):
        place = [lax.axis_index(axis) for axis in AXES]
        nx, ny, nz = self.counts
        mine = (place[0] * ny + place[1]) * nz + place[2]
        table = {}
        for link in FACES + RIMS:
            moved = [
                place[0] + (link // 9 - 1),
                place[1] + (link // 3 % 3 - 1),
                place[2] + (link % 3 - 1),
            ]
            inside = None
            for at, count in zip(moved, self.counts):
                here = jnp.logical_and(at >= 0, at < count)
                inside = here if inside is None else jnp.logical_and(inside, here)
            there = (moved[0] * ny + moved[1]) * nz + moved[2]
            table[link] = jnp.where(inside, there, mine)
        return table


def slot_row(layout, peer):
    empty = 1 << 20
    pieces_of = [peer[link : link + 1, : layout.slots] for link in FACES]
    pieces_of += [peer[link : link + 1, : layout.rim] for link in RIMS]
    used = len(FACES) * layout.slots + len(RIMS) * layout.rim
    pieces_of.append(jnp.full((1, layout.lanes - used), empty, jnp.int32))
    return jnp.concatenate(pieces_of, axis=1)


def swap_parts(layout, blocks):
    parts = layout.parts
    rows = blocks[0].shape[0]
    part = lax.broadcasted_iota(jnp.int32, (rows, LANES), 1) // layout.slots
    result = []
    for band in range(parts):
        tile = None
        for group in range(parts):
            shift = (layout.slots * (group - band)) % LANES
            moved = blocks[group]
            if shift:
                moved = pltpu.roll(moved, shift, 1)
            tile = moved if tile is None else jnp.where(part == group, moved, tile)
        result.append(tile)
    return result


def send(layout, table, values, send_ref, at):
    tiles = []
    for column in range(layout.columns):
        lanes = slice(column * LANES, (column + 1) * LANES)
        blocks = [
            values[group * layout.rows : (group + 1) * layout.rows, lanes]
            for group in range(layout.parts)
        ]
        tiles += swap_parts(layout, blocks)
    for link in FACES + RIMS:
        send_ref[table[link], at * layout.rows : (at + 1) * layout.rows, :] = tiles[
            layout.band_of(link)
        ]


def receive(layout, table, got_ref, at):
    rows = slice(at * layout.rows, (at + 1) * layout.rows)
    lane = lax.broadcasted_iota(jnp.int32, (layout.rows, LANES), 1)
    place = lane % layout.slots // layout.rim
    tiles = [got_ref[table[link], rows, :] for link in FACES]
    for start in range(0, len(RIMS), layout.per_group):
        tile = None
        for index, link in enumerate(RIMS[start : start + layout.per_group]):
            block = got_ref[table[link], rows, :]
            tile = block if tile is None else jnp.where(place == index ^ 1, block, tile)
        up = pltpu.roll(tile, layout.rim, 1)
        down = pltpu.roll(tile, LANES - layout.rim, 1)
        tiles.append(jnp.where(place % 2 == 1, up, down))
    while len(tiles) < layout.columns * layout.parts:
        tiles.append(jnp.zeros((layout.rows, LANES), F32))
    columns = []
    for column in range(layout.columns):
        blocks = swap_parts(layout, tiles[column * layout.parts : (column + 1) * layout.parts])
        columns.append(jnp.concatenate(blocks, axis=0))
    return jnp.concatenate(columns, axis=1)


def pieces(values):
    high = values.astype(BF16)
    low = (values - high.astype(F32)).astype(BF16)
    return high, low


def dot(left, right):
    return jnp.dot(left, right, preferred_element_type=F32)


def exact(left, right):
    return jnp.dot(left, right, precision=lax.Precision.HIGHEST, preferred_element_type=F32)


def prepared(weight):
    high = weight.astype(BF16).astype(F32)
    return jnp.concatenate([high, weight - high, high], axis=1).astype(BF16)


def weigh(weight, values):
    high, low = pieces(values)
    return dot(weight, jnp.concatenate([high, high, low], axis=0))


def sigmoid(values):
    return 0.5 * jnp.tanh(0.5 * values) + 0.5


def silu(values):
    return values * sigmoid(values)


def silu_slope(values):
    gate = sigmoid(values)
    return gate * (1.0 + values * (1.0 - gate))


def one_hots(indices):
    count = indices.shape[1]
    places = jnp.where(indices < 0, -1, indices % BLOCK).astype(F32)
    across = jnp.concatenate([jnp.broadcast_to(places, (16, count)).astype(BF16)] * (BLOCK // 16), axis=0)
    rows = lax.broadcasted_iota(jnp.int32, (BLOCK, count), 0).astype(F32).astype(BF16)
    down = jnp.broadcast_to(places, (LANES, count)).T.astype(BF16)
    down = jnp.concatenate([down] * (BLOCK // LANES), axis=1)
    lanes = lax.broadcasted_iota(jnp.int32, (count, BLOCK), 1).astype(F32).astype(BF16)
    one, zero = jnp.ones((), BF16), jnp.zeros((), BF16)
    return jnp.where(rows == across, one, zero), jnp.where(lanes == down, one, zero)


def gather_rows(values):
    high, low = pieces(values)
    rows = []
    for start in range(0, values.shape[1], BLOCK):
        rows += [high[:, start : start + BLOCK], low[:, start : start + BLOCK]]
    return jnp.concatenate(rows, axis=0)


def pick(found, indices, width):
    result = None
    for block in range(found.shape[0] // (2 * width)):
        at = 2 * width * block
        value = found[at : at + width] + found[at + width : at + 2 * width]
        result = value if result is None else jnp.where(indices >= block * BLOCK, value, result)
    return result


def gather(values, hot, indices):
    return pick(dot(gather_rows(values), hot), indices, values.shape[0])


def block_rows(values, indices, blocks):
    high, low = pieces(values)
    rows = []
    for block in range(blocks):
        inside = jnp.logical_and(indices >= block * BLOCK, indices < (block + 1) * BLOCK)
        mask = jnp.broadcast_to(jnp.where(inside, 1.0, 0.0), (16, indices.shape[1])).astype(BF16)
        mask = jnp.concatenate([mask] * (values.shape[0] // 16), axis=0)
        rows += [high * mask, low * mask]
    return jnp.concatenate(rows, axis=0)


def unblocked(summed, width):
    columns = []
    for at in range(0, summed.shape[0], 2 * width):
        columns.append(summed[at : at + width] + summed[at + width : at + 2 * width])
    return jnp.concatenate(columns, axis=1)


def scatter(values, tall, indices, blocks):
    return unblocked(dot(block_rows(values, indices, blocks), tall), values.shape[0])


def add(total, term):
    return term if total is None else total + term


def edges_forward(ends, edges_ref, hot_ref, tall_ref, pre_ref):
    width, nodes = ends.shape[0] // 2, ends.shape[1]
    left = gather_rows(ends[:width]), gather_rows(ends[width:])
    total = None
    for start in range(0, edges_ref.shape[1], CHUNK):
        span = slice(start, start + CHUNK)
        pre = None
        for side in range(2):
            found = dot(left[side], hot_ref[side, :, span])
            pre = add(pre, pick(found, edges_ref[side : side + 1, span], width))
        pre_ref[:, span] = pre
        rows = block_rows(silu(pre), edges_ref[1:2, span], nodes // BLOCK)
        total = add(total, dot(rows, tall_ref[1, span, :]))
    return unblocked(total, width)


def edges_backward(pulled, edges_ref, hot_ref, tall_ref, pre_ref):
    width, nodes = pulled.shape
    left = gather_rows(pulled)
    totals = [None, None]
    for start in range(0, edges_ref.shape[1], CHUNK):
        span = slice(start, start + CHUNK)
        found = dot(left, hot_ref[1, :, span])
        delta = pick(found, edges_ref[1:2, span], width) * silu_slope(pre_ref[:, span])
        for side in range(2):
            rows = block_rows(delta, edges_ref[side : side + 1, span], nodes // BLOCK)
            totals[side] = add(totals[side], dot(rows, tall_ref[side, span, :]))
    return jnp.concatenate([unblocked(total, width) for total in totals], axis=0)


def first_kernel(
    layout, opened_ref, features_ref, lists_ref, peer_ref, edge_in_ref, edge_out_ref,
    node_in_ref, node_out_ref, grad_ref,
    field_ref, cotangent_ref, edges_ref, hot_ref, tall_ref, slots_ref, slot_hot_ref, slot_tall_ref, base_ref, pulled_ref,
    pre_ref, joined_ref, send_ref,
    weight_1_ref, weight_2_ref, weight_3_ref, weight_4_ref, weight_5_ref, weight_6_ref,
    weight_7_ref, weight_8_ref,
):
    table = layout.neighbours()
    width, nodes = field_ref.shape
    field_ref[...] = features_ref[...]
    cotangent_ref[...] = grad_ref[...]
    edges_ref[...] = lists_ref[...]
    for side in range(2):
        for start in range(0, edges_ref.shape[1], CHUNK):
            span = slice(start, start + CHUNK)
            indices = lists_ref[side : side + 1, span]
            hot, tall = one_hots(jnp.where(indices < nodes, indices, -1))
            hot_ref[side, :, span] = hot
            tall_ref[side, span, :] = tall
    slots = slot_row(layout, peer_ref[...])
    slots = jnp.where(slots < nodes, slots, -1)
    slots_ref[...] = jnp.broadcast_to(slots, slots_ref.shape)
    slot_hot_ref[...], slot_tall_ref[...] = one_hots(slots)
    edge_1, edge_2 = edge_in_ref[0], edge_in_ref[1]
    node_1, node_2 = node_in_ref[0], node_in_ref[1]
    out_1, out_2 = node_out_ref[0], node_out_ref[1]
    ends_1 = jnp.concatenate([edge_1[:, :width], edge_1[:, width:]], axis=0)
    after = jnp.concatenate([edge_2[:, :width], edge_2[:, width:], node_2[:, :width]], axis=0)
    from_field = prepared(jnp.concatenate([ends_1, node_1[:, :width], after], axis=0))
    moved = weigh(from_field, features_ref[...])
    base_ref[...] = moved[2 * width :]
    join_1 = exact(node_1[:, width:], edge_out_ref[0])
    summed = edges_forward(moved[: 2 * width], lists_ref, hot_ref, tall_ref, pre_ref)
    joined = weigh(prepared(join_1), summed)
    joined_ref[...] = joined
    send(layout, table, gather(joined, slot_hot_ref[...], slots), send_ref, 0)
    join_2 = exact(node_2[:, width:], edge_out_ref[1])
    after_out = exact(after, out_1)
    weight_1_ref[...] = prepared(jnp.concatenate([out_1, after_out], axis=0))
    weight_2_ref[...] = prepared(join_2)
    weight_3_ref[...] = prepared(out_2)
    weight_4_ref[...] = prepared(join_2.T)
    back = jnp.concatenate(
        [jnp.concatenate([after, after_out], axis=1), jnp.zeros((width, 2 * width), F32)], axis=0
    ).T
    weight_5_ref[...] = prepared(back[:, : 2 * width])
    weight_6_ref[...] = prepared(back[:, 2 * width : 3 * width])
    weight_7_ref[...] = prepared(
        jnp.concatenate([join_1.T, node_1[:, :width].T], axis=0)
    )
    weight_8_ref[...] = prepared(ends_1.T)
    pulls = prepared(jnp.concatenate([out_1.T, out_2.T], axis=0))
    pulled_ref[...] = weigh(pulls, grad_ref[...])


def second_kernel(
    layout, got_ref, joined_ref, field_ref, base_ref, pulled_ref, edges_ref, hot_ref, tall_ref,
    slots_ref, slot_hot_ref, slot_tall_ref, weight_1_ref, weight_2_ref,
    node_pre_ref, next_ref, own_ref, pre_ref, next_joined_ref, at_slots_ref, send_ref,
):
    width, nodes = field_ref.shape
    table = layout.neighbours()
    slots, slot_hot, slot_tall = slots_ref[0:1], slot_hot_ref[...], slot_tall_ref[...]
    arrived = receive(layout, table, got_ref, 0)
    joined = joined_ref[...] + scatter(arrived, slot_tall, slots, nodes // BLOCK)
    node_pre = base_ref[:width] + joined
    node_pre_ref[...] = node_pre
    changes = weigh(weight_1_ref[...], silu(node_pre))
    next_ref[...] = field_ref[...] + changes[:width]
    moved = base_ref[width:] + changes[width:]
    own_ref[...] = moved[2 * width :]
    summed = edges_forward(moved[: 2 * width], edges_ref, hot_ref, tall_ref, pre_ref)
    joined = weigh(weight_2_ref[...], summed)
    next_joined_ref[...] = joined
    at_slots = gather(joined, slot_hot, slots)
    at_slots_ref[...] = at_slots
    send(layout, table, at_slots, send_ref, 0)
    send(layout, table, gather(moved[2 * width :], slot_hot, slots), send_ref, 1)
    send(layout, table, gather(pulled_ref[width:], slot_hot, slots), send_ref, 2)


def third_kernel(
    layout, got_ref, joined_ref, at_slots_ref, field_ref, cotangent_ref, own_ref, pulled_ref,
    pre_ref, node_pre_ref, edges_ref, hot_ref, tall_ref, slots_ref, slot_hot_ref, slot_tall_ref,
    weight_3_ref, weight_4_ref, weight_5_ref, weight_6_ref, weight_7_ref,
    updated_ref, field_grad_ref, joined_grad_ref, send_ref,
):
    width, nodes = field_ref.shape
    table = layout.neighbours()
    slots, slot_hot, slot_tall = slots_ref[0:1], slot_hot_ref[...], slot_tall_ref[...]
    arrived = receive(layout, table, got_ref, 0)
    peer_pre = receive(layout, table, got_ref, 1) + (at_slots_ref[...] + arrived)
    peer_delta = receive(layout, table, got_ref, 2) * silu_slope(peer_pre)
    joined = joined_ref[...] + scatter(arrived, slot_tall, slots, nodes // BLOCK)
    node_pre = own_ref[...] + joined
    updated_ref[...] = field_ref[...] + weigh(weight_3_ref[...], silu(node_pre))
    delta = pulled_ref[width:] * silu_slope(node_pre)
    both = delta + scatter(peer_delta, slot_tall, slots, nodes // BLOCK)
    summed = edges_backward(weigh(weight_4_ref[...], both), edges_ref, hot_ref, tall_ref, pre_ref)
    changes = weigh(weight_5_ref[...], summed) + weigh(weight_6_ref[...], delta)
    upstream = cotangent_ref[...] + changes[:width]
    delta = (pulled_ref[:width] + changes[width:]) * silu_slope(node_pre_ref[...])
    back = weigh(weight_7_ref[...], delta)
    joined_grad_ref[...] = back[:width]
    send(layout, table, gather(back[:width], slot_hot, slots), send_ref, 0)
    field_grad_ref[...] = upstream + back[width:]


def fourth_kernel(
    layout, got_ref, joined_grad_ref, field_grad_ref, pre_ref, edges_ref, hot_ref, tall_ref, slots_ref,
    slot_tall_ref, weight_8_ref, grad_ref,
):
    nodes = joined_grad_ref.shape[1]
    table = layout.neighbours()
    arrived = receive(layout, table, got_ref, 0)
    pulled = joined_grad_ref[...] + scatter(
        arrived, slot_tall_ref[...], slots_ref[0:1], nodes // BLOCK
    )
    summed = edges_backward(pulled, edges_ref, hot_ref, tall_ref, pre_ref)
    grad_ref[...] = field_grad_ref[...] + weigh(weight_8_ref[...], summed)


def opening_kernel(opened_ref):
    opened_ref[...] = jnp.zeros(opened_ref.shape, jnp.int32)


def call(kernel, layout, shapes, arrays):
    return pl.pallas_call(
        functools.partial(kernel, layout),
        out_shape=[jax.ShapeDtypeStruct(shape, kind) for shape, kind in shapes],
        in_specs=[pl.BlockSpec(memory_space=pltpu.VMEM)] * len(arrays),
        out_specs=[pl.BlockSpec(memory_space=pltpu.VMEM)] * len(shapes),
        compiler_params=pltpu.CompilerParams(vmem_limit_bytes=40 << 20),
    )(*arrays)


def exchanged(blocks):
    return lax.all_to_all(blocks, AXES, 0, 0)


def on_device(counts, features, edge_lists, peer_nodes, edge_in, edge_out, node_in, node_out, cotangent):
    width, nodes = features.shape
    edges = edge_lists.shape[1]
    layout = Layout(width, peer_nodes.shape[1], counts)
    rows, devices, lanes = layout.rows, layout.devices, layout.lanes
    like = lambda times: ((times * width, nodes), F32)
    edge_like = ((width, edges), F32)
    weight = lambda tall, wide: ((tall * width, 3 * wide * width), BF16)
    sent = lambda times: ((devices, times * rows, LANES), F32)
    opened = pl.pallas_call(
        opening_kernel,
        out_shape=jax.ShapeDtypeStruct((8, LANES), jnp.int32),
        out_specs=pl.BlockSpec(memory_space=pltpu.VMEM),
        cost_estimate=pl.CostEstimate(flops=10**10, bytes_accessed=10**7, transcendentals=0),
        compiler_params=pltpu.CompilerParams(vmem_limit_bytes=1 << 20),
    )()
    (field, pull, lists, hot, tall, slots, slot_hot, slot_tall, base, pulled, pre_1, joined, blocks,
     *weights) = call(
        first_kernel, layout,
        [like(1), like(1), ((2, edges), jnp.int32), ((2, BLOCK, edges), BF16),
         ((2, edges, BLOCK), BF16), ((8, lanes), jnp.int32), ((BLOCK, lanes), BF16),
         ((lanes, BLOCK), BF16), like(4), like(2), edge_like, like(1),
         sent(1),
         weight(4, 1), weight(1, 1), weight(1, 1), weight(1, 1), weight(2, 2), weight(2, 1),
         weight(2, 1), weight(1, 2)],
        [opened, features, edge_lists, peer_nodes, edge_in, edge_out, node_in, node_out, cotangent],
    )
    got = exchanged(blocks)
    node_pre, next_field, own, pre_2, joined, at_slots, blocks = call(
        second_kernel, layout,
        [like(1), like(1), like(1), edge_like, like(1), ((width, lanes), F32), sent(3)],
        [got, joined, field, base, pulled, lists, hot, tall, slots, slot_hot, slot_tall,
         weights[0], weights[1]],
    )
    got = exchanged(blocks)
    updated, field_grad, joined_grad, blocks = call(
        third_kernel, layout,
        [like(1), like(1), like(1), sent(1)],
        [got, joined, at_slots, next_field, pull, own, pulled, pre_2, node_pre, lists, hot, tall,
         slots, slot_hot, slot_tall, *weights[2:7]],
    )
    got = exchanged(blocks)
    (feature_grad,) = call(
        fourth_kernel, layout, [like(1)],
        [got, joined_grad, field_grad, pre_1, lists, hot, tall, slots, slot_tall, weights[7]],
    )
    return updated, feature_grad


def solution(mesh):
    split = P(None, AXES)
    counts = tuple(mesh.shape[axis] for axis in AXES)
    return jax.shard_map(
        functools.partial(on_device, counts),
        mesh=mesh,
        in_specs=(split, split, split, P(), P(), P(), P(), split),
        out_specs=(split, split),
        check_vma=False,
    )
```
